128 devices in a mesh: px: 8 (over y, core), py: 16 (over x, z).
Axes of the slice: x: 4, y: 4, z: 4, core: 2. Of those that a mesh axis runs over, the one named last changes fastest.
Arguments:
- coupling_vals: float32 [32, 64, 9, 64, 64], P('px', 'py'), may hold values from -0.75 to 0.75
- coupling_cols: int32 [32, 64, 9], P('px', 'py'), may hold values from 0 to 2047, as said below
- coupling_len: int32 [32, 64], P('px', 'py'), may hold values from 1 to 9
- interp_vals: float32 [32, 64, 4, 64, 64], P('px', 'py'), may hold values from -0.75 to 0.75
- interp_cols: int32 [32, 64, 4], P('px', 'py'), may hold values from 0 to 511, as said below
- interp_len: int32 [32, 64], P('px', 'py'), may hold values from 1 to 4
- owner_map: int32 [8, 16, 4, 1], P('px'), may hold values from 0 to 15; in each aligned block of 4 rows (0 to 3, 4 to 7, ..., all dimensions but the last counted through in order) at most 2 rows name the same one
Outputs:
- relayed_rows: float32 [4096, 25, 64, 64], P(('px', 'py'))
- relayed_ids: int32 [4096], P(('px', 'py'))
The draws below stay inside these ranges and needn't reach their ends.
Inputs may be any that keep to these rules, and one draw needn't show every extreme that they name: `coupling_cols`: row (x, y) names in its first coupling_len[x, y] slots distinct fine blocks x' 64 + y' of the grid with x' - x and y' - y each in -1, 0, 1; later slots name the row's own block. `interp_cols`: row (x, y) names in its first interp_len[x, y] slots distinct coarse blocks X 32 + Y of the coarse grid with X - x div 2 and Y - y div 2 each 0 or 1; later slots name (x div 2) * 32 + y div 2. `owner_map`: among the 4 entries of one grid device, no value appears more than 2 times.
All inputs are finite; a program needn't handle non-finite values.
Results may differ from the reference program's by a relative error of at most 0.0003.
Values sent between devices are 32-bit elements; how exact they have to be, the bound alone decides.
No kernel may reach another device: no remote copies, remote signals or barrier semaphores. Data moves between devices by JAX's collectives and lax.ppermute only.
A program may use at most 256 MiB of HBM per device.

```python
import math
import jax
import jax.numpy as jnp
import numpy as np
from jax import lax

BLOCK = 64
AGG_X = 2
AGG_Y = 2
CAP = 2
FX = 32
FY = 64
CX = 16
CY = 32
N_PX = 8
N_PY = 16


def coupling_pattern(key):
    key = jax.random.fold_in(key, 11)
    key_order, key_drop = jax.random.split(key)
    offsets = jnp.arange(9, dtype=jnp.int32)
    row_x = jnp.arange(FX, dtype=jnp.int32)[:, None, None]
    row_y = jnp.arange(FY, dtype=jnp.int32)[None, :, None]
    near_x = jnp.broadcast_to(row_x + offsets // 3 - 1, (FX, FY, 9))
    near_y = jnp.broadcast_to(row_y + offsets % 3 - 1, (FX, FY, 9))
    inside = (near_x >= 0) & (near_x < FX) & (near_y >= 0) & (near_y < FY)
    ranking = jax.random.randint(key_order, (FX, FY, 9), 0, 4096) * 16 + offsets
    ranking = jnp.where(inside, ranking, ranking + 100000)
    ranked = jnp.argsort(ranking, axis=-1)
    chosen = jnp.take_along_axis(near_x * FY + near_y, ranked, axis=-1)
    valid_count = jnp.sum(inside.astype(jnp.int32), axis=-1)
    dropped = jax.random.randint(key_drop, (FX, FY), 0, 3)
    full_rows = (row_x[:, :, 0] % 4 == 1) & (row_y[:, :, 0] % 4 == 1)
    dropped = jnp.where(full_rows, 0, dropped)
    length = jnp.maximum(valid_count - dropped, 1).astype(jnp.int32)
    own_block = row_x * FY + row_y
    slot_ids = jnp.arange(9, dtype=jnp.int32)
    columns = jnp.where(slot_ids < length[:, :, None], chosen, own_block)
    return (columns.astype(jnp.int32), length)


def interp_pattern(key):
    key = jax.random.fold_in(key, 23)
    key_order, key_drop = jax.random.split(key)
    offsets = jnp.arange(4, dtype=jnp.int32)
    row_x = jnp.arange(FX, dtype=jnp.int32)[:, None, None]
    row_y = jnp.arange(FY, dtype=jnp.int32)[None, :, None]
    target_x = jnp.broadcast_to(row_x // 2 + offsets // 2, (FX, FY, 4))
    target_y = jnp.broadcast_to(row_y // 2 + offsets % 2, (FX, FY, 4))
    inside = (target_x < CX) & (target_y < CY)
    ranking = jax.random.randint(key_order, (FX, FY, 4), 0, 4096) * 8 + offsets
    ranking = jnp.where(inside, ranking, ranking + 100000)
    ranked = jnp.argsort(ranking, axis=-1)
    chosen = jnp.take_along_axis(target_x * CY + target_y, ranked, axis=-1)
    valid_count = jnp.sum(inside.astype(jnp.int32), axis=-1)
    dropped = jax.random.randint(key_drop, (FX, FY), 0, 2)
    full_rows = (row_x[:, :, 0] % 4 == 1) & (row_y[:, :, 0] % 4 == 1)
    dropped = jnp.where(full_rows, 0, dropped)
    length = jnp.maximum(valid_count - dropped, 1).astype(jnp.int32)
    own_block = row_x // 2 * CY + row_y // 2
    slot_ids = jnp.arange(4, dtype=jnp.int32)
    columns = jnp.where(slot_ids < length[:, :, None], chosen, own_block)
    return (columns.astype(jnp.int32), length)


def draw_coupling_cols(key, part):
    return coupling_pattern(key)[0]


def draw_coupling_len(key, part):
    return coupling_pattern(key)[1]


def draw_interp_cols(key, part):
    return interp_pattern(key)[0]


def draw_interp_len(key, part):
    return interp_pattern(key)[1]


def level_of(key, shape, cuts, low, top_value):
    def one(axis_at, blocks):
        steps = jax.random.uniform(jax.random.fold_in(jax.random.fold_in(key, 6), axis_at), (blocks,), jnp.float32, low / len(cuts), top_value / len(cuts))
        return jnp.repeat(jnp.exp(steps), shape[axis_at] // blocks).reshape((-1,) + (1,) * (len(shape) - axis_at - 1))

    level = one(*cuts[0])
    for cut in cuts[1:]:
        level = level * one(*cut)
    return level


def routed_block(rng, own, number, rows, count, top, most, skew):
    sequence = jax.random.permutation(rng, count)
    packed, ordinary = portions_of(count, rows * top, most, skew, True), portions_of(count, rows * top, most, skew, False)
    places = jnp.arange(count)

    def named(sizes, rotation):
        used = int((sizes > 0).sum())
        fixed = max(1, used // 4)
        passed = fixed + (places - fixed + rotation * (used - fixed)) % max(1, count - fixed)
        return jnp.zeros((count,), jnp.int32).at[sequence[jnp.where(places < fixed, places, passed)]].set(jnp.asarray(sizes, jnp.int32))

    sizes = jnp.where(number % 4 == 0, named(packed, number // 4), named(ordinary, number - number // 4 - 1))
    mixed = jax.random.permutation(jax.random.fold_in(own, 3), count)
    donor, taker = mixed[0:count // 2 * 2:2], mixed[1:count // 2 * 2:2]
    room = jnp.minimum(sizes[donor] - 1, most - sizes[taker]) // 2
    room = jnp.where((donor == sequence[0]) | (taker == sequence[0]) | (sizes[taker] == 0), 0, jnp.maximum(room, 0))
    passed = jax.random.randint(jax.random.fold_in(own, 4), (count // 2,), 0, 1 << 20) % (room + 1)
    sizes = sizes.at[donor].add(-passed).at[taker].add(passed)
    members = jnp.searchsorted(jnp.cumsum(sizes), jnp.arange(rows * top), side="right").astype(jnp.int32)
    listing = members.reshape(top, rows).T
    listing = listing[jax.random.permutation(jax.random.fold_in(own, 1), rows)]
    rotation = jax.random.randint(jax.random.fold_in(own, 2), (rows, 1), 0, top)
    return jnp.take_along_axis(listing, (jnp.arange(top)[None, :] + rotation) % top, axis=1)


def portions_of(amount, total, most, skew, full):
    weights = [(1 << 20) // math.isqrt(standing ** skew) + 1 for standing in range(1, amount + 1)]
    largest = most if full else min(most, max(-(-total // amount), total * weights[0] // sum(weights)))
    least = 1 if total - largest >= amount - 1 else 0
    given, rest = [largest] + [least] * (amount - 1), total - largest - least * (amount - 1)
    while rest > 0:
        free = [i for i in range(1, amount) if given[i] < largest] or [i for i in range(1, amount) if given[i] < most]
        pool, left = sum([weights[i] for i in free]), rest
        for i in free:
            extra = min(most - given[i], max(1, left * weights[i] // pool), rest)
            given[i] = given[i] + extra
            rest = rest - extra
    return np.array(given)


def bell_draw(stream_key, shape, scale, limit, cuts=(), kind=jnp.bfloat16):
    values = scale * jax.random.normal(stream_key, shape, jnp.float32)
    if cuts:
        values = values * level_of(stream_key, shape, cuts, -0.22, 0.18)
    return jnp.clip(values, -limit, limit).astype(kind)


def setup_inputs(seed: int = 0) -> dict:
    arg_keys = jax.random.split(jax.random.key(seed), 8)
    coupling_vals = bell_draw(arg_keys[0], (FX, FY, 9, BLOCK, BLOCK), BLOCK ** -0.5, 0.75, ((0, 8), (1, 16)), jnp.float32)
    coupling_cols = draw_coupling_cols(jax.random.fold_in(arg_keys[7], 71), 0)
    coupling_len = draw_coupling_len(jax.random.fold_in(arg_keys[7], 71), 0)
    interp_vals = bell_draw(arg_keys[3], (FX, FY, 4, BLOCK, BLOCK), BLOCK ** -0.5, 0.75, ((0, 8), (1, 16)), jnp.float32)
    interp_cols = draw_interp_cols(jax.random.fold_in(arg_keys[7], 71), 0)
    interp_len = draw_interp_len(jax.random.fold_in(arg_keys[7], 71), 0)
    owner_map_keys = jax.random.split(jax.random.fold_in(arg_keys[6], 1), N_PX * N_PY * (AGG_X * AGG_Y) // (AGG_X * AGG_Y))
    owner_map_turns = jax.random.permutation(jax.random.fold_in(arg_keys[6], 3), N_PX * N_PY * (AGG_X * AGG_Y) // (AGG_X * AGG_Y))
    owner_map = jax.vmap(lambda own, number: routed_block(jax.random.fold_in(arg_keys[6], 2), own, number, AGG_X * AGG_Y, N_PY, 1, CAP, 2))(owner_map_keys, owner_map_turns).reshape((N_PX, N_PY, AGG_X * AGG_Y, 1))
    return {"coupling_vals": coupling_vals, "coupling_cols": coupling_cols, "coupling_len": coupling_len, "interp_vals": interp_vals, "interp_cols": interp_cols, "interp_len": interp_len, "owner_map": owner_map}


def fold_table(parity_x, parity_y):
    table = np.zeros((36, 16), np.float32)
    for offset in range(9):
        step_x = offset // 3 - 1
        step_y = offset % 3 - 1
        for corner in range(4):
            target_x = (parity_x + step_x) // 2 + corner // 2 + 1
            target_y = (parity_y + step_y) // 2 + corner % 2 + 1
            table[offset * 4 + corner, target_x * 4 + target_y] = 1.0
    return table


def dense_coupling(values, columns, lengths, row_x, row_y, fine_y):
    column_x = columns // fine_y
    column_y = columns % fine_y
    offset = (column_x - row_x + 1) * 3 + (column_y - row_y + 1)
    slot_ids = jnp.arange(9, dtype=jnp.int32)
    live = slot_ids < lengths[:, :, None]
    select = (offset[..., None] == slot_ids) & live[..., None]
    return jnp.einsum("xysc,xysab->xycab", select.astype(values.dtype), values, precision=lax.Precision.HIGHEST)


def dense_interp(values, columns, lengths, row_x, row_y, coarse_y):
    offset = (columns // coarse_y - row_x // 2) * 2 + (columns % coarse_y - row_y // 2)
    slot_ids = jnp.arange(4, dtype=jnp.int32)
    live = slot_ids < lengths[:, :, None]
    select = (offset[..., None] == slot_ids) & live[..., None]
    return jnp.einsum("xysc,xysab->xycab", select.astype(values.dtype), values, precision=lax.Precision.HIGHEST)


def galerkin_terms(operator_blocks, interp_cycle):
    span_x = operator_blocks.shape[0] // 2
    span_y = operator_blocks.shape[1] // 2
    width = operator_blocks.shape[-1]
    merged_list = []
    own_list = []
    for parity_x in (0, 1):
        for parity_y in (0, 1):
            fine_rows = operator_blocks[parity_x::2, parity_y::2]
            pieces = []
            for step_x in (-1, 0, 1):
                for step_y in (-1, 0, 1):
                    begin_x = 1 + parity_x + step_x
                    begin_y = 1 + parity_y + step_y
                    pieces.append(interp_cycle[begin_x:begin_x + 2 * span_x:2, begin_y:begin_y + 2 * span_y:2])
            neighbours = jnp.stack(pieces, axis=2)
            products = jnp.einsum("xycab,xycqbd->xycqad", fine_rows, neighbours, precision=lax.Precision.HIGHEST)
            products = products.reshape(span_x, span_y, 36, width, width)
            table = jnp.asarray(fold_table(parity_x, parity_y), products.dtype)
            merged_list.append(jnp.einsum("xykad,kn->xynad", products, table, precision=lax.Precision.HIGHEST))
            own_list.append(interp_cycle[1 + parity_x:1 + parity_x + 2 * span_x:2, 1 + parity_y:1 + parity_y + 2 * span_y:2])
    blocks = jnp.einsum("kxypba,kxynbc->xypnac", jnp.stack(own_list), jnp.stack(merged_list), precision=lax.Precision.HIGHEST)
    accumulated = jnp.zeros((span_x + 1, span_y + 1, 25, width, width), blocks.dtype)
    for corner in range(4):
        high_x = corner // 2
        high_y = corner % 2
        placed = blocks[:, :, corner].reshape(span_x, span_y, 4, 4, width, width)
        placed = jnp.pad(placed, ((high_x, 1 - high_x), (high_y, 1 - high_y), (1 - high_x, high_x), (1 - high_y, high_y), (0, 0), (0, 0)))
        accumulated = accumulated + placed.reshape(span_x + 1, span_y + 1, 25, width, width)
    return accumulated


def reference(coupling_vals, coupling_cols, coupling_len, interp_vals, interp_cols, interp_len, owner_map):
    fine_x = coupling_cols.shape[0]
    fine_y = coupling_cols.shape[1]
    coarse_x = fine_x // 2
    coarse_y = fine_y // 2
    width = coupling_vals.shape[-1]
    row_x = jnp.arange(fine_x, dtype=jnp.int32)[:, None, None]
    row_y = jnp.arange(fine_y, dtype=jnp.int32)[None, :, None]
    interp_all = dense_interp(interp_vals, interp_cols, interp_len, row_x, row_y, coarse_y)
    interp_all = jnp.pad(interp_all, ((1, 1), (1, 1), (0, 0), (0, 0), (0, 0)))

    def sweep(carry, agg_index):
        start = 2 * agg_index
        slab_x = start + jnp.arange(2, dtype=jnp.int32)[:, None, None]
        operator_blocks = dense_coupling(
            lax.dynamic_slice_in_dim(coupling_vals, start, 2, 0),
            lax.dynamic_slice_in_dim(coupling_cols, start, 2, 0),
            lax.dynamic_slice_in_dim(coupling_len, start, 2, 0),
            slab_x, row_y, fine_y)
        interp_cycle = lax.dynamic_slice_in_dim(interp_all, start, 4, 0)
        terms = galerkin_terms(operator_blocks, interp_cycle)
        return terms[1, :coarse_y], carry + terms[0, :coarse_y]

    initial = jnp.zeros((coarse_y, 25, width, width), jnp.float32)
    leftover, coarse = lax.scan(sweep, initial, jnp.arange(coarse_x, dtype=jnp.int32))
    per_device = AGG_X * AGG_Y
    grid_rows = coarse.reshape(N_PX, AGG_X, N_PY, AGG_Y, 25, width, width)
    grid_rows = grid_rows.transpose(0, 2, 1, 3, 4, 5, 6).reshape(N_PX * N_PY * per_device, 25, width, width)
    target = owner_map[:, :, :, 0]
    hits = (target[..., None] == jnp.arange(N_PY, dtype=jnp.int32)).astype(jnp.int32)
    before = jnp.cumsum(hits, axis=2) - hits
    rank = jnp.sum(before * hits, axis=-1)
    device_x = jnp.arange(N_PX, dtype=jnp.int32)[:, None, None]
    device_y = jnp.arange(N_PY, dtype=jnp.int32)[None, :, None]
    slot = ((device_x * N_PY + target) * N_PY + device_y) * CAP + rank
    local = jnp.arange(per_device, dtype=jnp.int32)[None, None, :]
    ident = (device_x * AGG_X + local // AGG_Y) * coarse_y + device_y * AGG_Y + local % AGG_Y
    total_slots = N_PX * N_PY * N_PY * CAP
    relayed_rows = jnp.zeros((total_slots, 25, width, width), coarse.dtype).at[slot.reshape(-1)].set(grid_rows)
    relayed_ids = jnp.full((total_slots,), -1, jnp.int32).at[slot.reshape(-1)].set(ident.reshape(-1).astype(jnp.int32))
    return relayed_rows, relayed_ids
```

```python
import jax
import jax.numpy as jnp
from jax import lax
from jax.experimental import pallas as pl
from jax.experimental.pallas import tpu as pltpu
from jax.sharding import PartitionSpec as P

CAP = 2
FAST_K = 6
FAST_E = 24
VM = pltpu.VMEM
SM = pltpu.SMEM
F32 = jnp.float32
BF16 = jnp.bfloat16
LIMIT = 60 * 1024 * 1024


def spec(space):
    return pl.BlockSpec(memory_space=space)


def params():
    return pltpu.CompilerParams(vmem_limit_bytes=LIMIT)


def split(value):
    high = value.astype(BF16)
    low = (value - high.astype(F32)).astype(BF16)
    return high, low


def dot3(left, right):
    out = jnp.dot(left[0], right[0], preferred_element_type=F32)
    out += jnp.dot(left[0], right[1], preferred_element_type=F32)
    out += jnp.dot(left[1], right[0], preferred_element_type=F32)
    return out


def interp_kernel(meta, cols, lens, vals, dense, west, east, south, north, corners, slots):
    coarse_y = meta[2] // 2
    slots[...] = jnp.zeros_like(slots)
    for x in range(4):
        for y in range(4):
            row_x = (meta[0] * 4 + x) // 2
            row_y = (meta[1] * 4 + y) // 2
            count = lens[x, y]
            for s in range(4):
                col = cols[x, y, s]
                place = (col % coarse_y - row_y) * 2 + (col // coarse_y - row_x)
                place = jnp.where(s < count, place, 4)
                slots[x * 4 + y, place] = vals[x, y, s]
    for x in range(4):
        for y in range(4):
            j = x * 4 + y
            block = jnp.concatenate([slots[j, q] for q in range(4)], axis=1)
            dense[j] = block
            if x == 0:
                west[y] = block
            if x == 3:
                east[y] = block
            if y == 0:
                south[x] = block
            if y == 3:
                north[x] = block
            if x in (0, 3) and y in (0, 3):
                corners[(x // 3) * 2 + y // 3] = block


def galerkin_kernel(
    meta, cols, lens, vals, dense, at_west, at_east, at_south, at_north, c00, c01, c10, c11,
    own, send, slots, phi, plo, wacc,
):
    fine_y = meta[2]
    slots[...] = jnp.zeros_like(slots)
    for x in range(4):
        for y in range(4):
            row_x = meta[0] * 4 + x
            row_y = meta[1] * 4 + y
            count = lens[x, y]
            for s in range(9):
                col = cols[x, y, s]
                place = (col // fine_y - row_x + 1) * 3 + (col % fine_y - row_y + 1)
                place = jnp.where(s < count, place, 9)
                slots[x * 4 + y, place] = vals[x, y, s]

    def interp_at(x, y):
        if 0 <= x < 4 and 0 <= y < 4:
            return dense[x * 4 + y]
        if 0 <= y < 4:
            return at_west[y] if x < 0 else at_east[y]
        if 0 <= x < 4:
            return at_south[x] if y < 0 else at_north[x]
        return {(-1, -1): c00, (-1, 4): c01, (4, -1): c10, (4, 4): c11}[(x, y)][...]

    for x in range(-1, 5):
        for y in range(-1, 5):
            n = (x + 1) * 6 + y + 1
            high, low = split(interp_at(x, y))
            phi[n] = high
            plo[n] = low
    own[...] = jnp.zeros_like(own)
    send[...] = jnp.zeros_like(send)
    for ax in range(2):
        for ay in range(2):
            wacc[...] = jnp.zeros_like(wacc)
            for dx in (-1, 0, 1):
                for dy in (-1, 0, 1):
                    lx = {-1: [0], 0: [0, 1], 1: [1]}[dx]
                    ly = {-1: [0], 0: [0, 1], 1: [1]}[dy]
                    jx = {-1: [-1], 0: [0, 1], 1: [2]}[dx]
                    jy = {-1: [-1], 0: [0, 1], 1: [2]}[dy]
                    fine_i = [(u, v) for u in lx for v in ly]
                    fine_j = [(u, v) for u in jx for v in jy]
                    left = jnp.concatenate(
                        [
                            jnp.concatenate(
                                [
                                    slots[
                                        (2 * ax + ix) * 4 + 2 * ay + iy,
                                        (u - ix + 1) * 3 + v - iy + 1,
                                    ]
                                    for u, v in fine_j
                                ],
                                axis=1,
                            )
                            for ix, iy in fine_i
                        ],
                        axis=0,
                    )
                    where = [(2 * ax + u + 1) * 6 + 2 * ay + v + 1 for u, v in fine_j]
                    right = (
                        jnp.concatenate([phi[n] for n in where], axis=0),
                        jnp.concatenate([plo[n] for n in where], axis=0),
                    )
                    product = dot3(split(left), right)
                    for n, (ix, iy) in enumerate(fine_i):
                        rows = slice((ix * 2 + iy) * 64, (ix * 2 + iy) * 64 + 64)
                        for qy in range(2):
                            at = ((dy + 1 + qy) * 4 + dx + 1) * 64
                            wacc[rows, at : at + 128] += product[
                                n * 64 : n * 64 + 64, qy * 128 : qy * 128 + 128
                            ]
            own_p = jnp.concatenate(
                [dense[(2 * ax + u) * 4 + 2 * ay + v] for u in range(2) for v in range(2)], axis=0
            )
            coarse = dot3(split(own_p.T), split(wacc[...]))
            for qy in range(2):
                for qx in range(2):
                    ix, iy = ax + qx, ay + qy
                    rows = slice((qy * 2 + qx) * 64, (qy * 2 + qx) * 64 + 64)
                    for ty in range(4):
                        piece = coarse[rows, ty * 256 : ty * 256 + 256]
                        if ix == 2:
                            at = (ty + 1 - qy) * 256
                            send[iy, :, at : at + 256] += piece
                        else:
                            at = ((ty + 1 - qy) * 5 + 1 - qx) * 64
                            own[ix * 3 + iy, :, at : at + 256] += piece


def half_tiles(piece, start, stop):
    return piece[:, start * 64 : stop * 64]


def pack_kernel(own, got, out, acc):
    for iy in range(3):
        acc[iy] = own[iy]
        for jy in range(5):
            acc[iy, :, jy * 320 : jy * 320 + 256] += got[iy, :, jy * 256 : jy * 256 + 256]
    for ix in range(2):
        row = [acc[iy] if ix == 0 else own[3 + iy] for iy in range(3)]
        for g in range(8):
            band = [r[g * 8 : g * 8 + 8] for r in row]
            out[2 * g, ix, :, 0:768] = half_tiles(band[1], 0, 12)
            out[2 * g, ix, :, 768:1536] = half_tiles(band[2], 0, 12)
            out[2 * g, ix, :, 1536:2048] = half_tiles(band[0], 4, 12)
            out[2 * g, ix, :, 2048:2176] = jnp.zeros((8, 128), F32)
            out[2 * g + 1, ix, :, 0:768] = half_tiles(band[1], 12, 24)
            out[2 * g + 1, ix, :, 768:1536] = half_tiles(band[0], 12, 24)
            out[2 * g + 1, ix, :, 1536:1664] = jnp.concatenate(
                [half_tiles(band[1], 24, 25), half_tiles(band[0], 24, 25)], axis=1
            )
            out[2 * g + 1, ix, :, 1664:2176] = half_tiles(band[2], 12, 20)


def route_kernel(kept, meta, owners, deliver, extra, source, plain, ids, need, count):
    peers = 16
    coarse_y = meta[2] // 2
    for e in range(peers):
        count[e] = 0
    for n in range(2 * peers):
        source[n] = -1
        plain[n] = -1
        ids[n] = -1

    def clear(n, carry):
        deliver[n] = 0
        return carry

    lax.fori_loop(0, peers * 32, clear, 0)

    def clear_extra(n, carry):
        extra[n] = 0
        return carry

    lax.fori_loop(0, 64, clear_extra, 0)

    def step(dy, spare):
        for k in range(4):
            e = owners[dy * 4 + k]
            rank = 0
            for before in range(k):
                rank += (owners[dy * 4 + before] == e).astype(jnp.int32)
            n = count[e]
            count[e] = n + 1
            deliver[e * 32 + n] = dy * 4 + k
            over = n >= kept
            here = jnp.where(over, kept + spare, n)
            extra[jnp.where(over, spare, 63)] = dy * 4 + k
            spare = jnp.where(over, spare + 1, spare)

            @pl.when(e == meta[1])
            def _():
                source[dy * 2 + rank] = here
                plain[dy * 2 + rank] = n
                ids[dy * 2 + rank] = (meta[0] * 2 + k // 2) * coarse_y + dy * 2 + k % 2

        return spare

    spare = lax.fori_loop(0, peers, step, 0)
    for n in range(8):
        need[n] = spare


def fan_kernel(kept, spare, meta, deliver, extra, got, *refs):
    out = refs[0]
    rows = refs[-1]
    half = meta[1] % 2

    @pl.when(half == 0)
    def _():
        def step(dy, carry):
            for ix in range(2):
                rows[dy * 4 + ix * 2, :, 0:256] = jnp.zeros((8, 256), F32)
                rows[dy * 4 + ix * 2, :, 256:768] = got[dy, ix, :, 1536:2048]
                rows[dy * 4 + ix * 2 + 1, :, 0:768] = got[dy, ix, :, 0:768]

                @pl.when(dy > 0)
                def _():
                    rows[dy * 4 + ix * 2, :, 0:768] += got[dy - 1, ix, :, 768:1536]

            return carry

        lax.fori_loop(0, 16, step, 0)

    @pl.when(half == 1)
    def _():
        def step(dy, carry):
            for ix in range(2):
                last = got[dy, ix, :, 1536:1664]
                rows[dy * 4 + ix * 2 + 1, :, 0:768] = got[dy, ix, :, 0:768]
                rows[dy * 4 + ix * 2 + 1, :, 768:896] = last
                rows[dy * 4 + ix * 2, :, 0:768] = got[dy, ix, :, 768:1536]
                rows[dy * 4 + ix * 2, :, 768:832] = last[:, 64:128]

                @pl.when(dy > 0)
                def _():
                    rows[dy * 4 + ix * 2, :, 0:512] += got[dy - 1, ix, :, 1664:2176]

            return carry

        lax.fori_loop(0, 16, step, 0)

    def place(e, carry):
        for n in range(kept):
            out[e, n] = rows[deliver[e * 32 + n]]
        return carry

    lax.fori_loop(0, 16, place, 0)
    for n in range(spare):
        refs[1][n] = rows[extra[n]]


def collect_kernel(kept, source, near, *refs):
    out = refs[-1]
    at = source[pl.program_id(0)]

    def write(get):
        for g in range(8):
            pair = (get(2 * g), get(2 * g + 1))
            for n in range(25):
                piece, lane = (pair[0], n) if n < 12 else (pair[1], n - 12)
                out[0, (n % 5) * 5 + n // 5, g * 8 : g * 8 + 8, :] = piece[
                    :, lane * 64 : lane * 64 + 64
                ]

    @pl.when(at < 0)
    def _():
        out[...] = jnp.zeros_like(out)

    @pl.when((at >= 0) & (at < kept))
    def _():
        write(lambda c: near[c, at])

    if len(refs) > 1:

        @pl.when(at >= kept)
        def _():
            write(lambda c: refs[0][c, at - kept])


def relay(kept, spare, meta, deliver, extra, source, got):
    outs = [jax.ShapeDtypeStruct((16, kept, 8, 896), F32)]
    if spare:
        outs.append(jax.ShapeDtypeStruct((spare, 8, 896), F32))
    fan = pl.pallas_call(
        lambda *refs: fan_kernel(kept, spare, *refs),
        out_shape=outs,
        in_specs=[spec(SM)] * 3 + [spec(VM)],
        out_specs=[spec(VM)] * len(outs),
        scratch_shapes=[VM((64, 8, 896), F32)],
        compiler_params=params(),
    )(meta, deliver, extra, got)
    args = []
    if spare:
        args = [lax.all_gather(fan[1], "py", axis=0, tiled=False)]
    args = [lax.all_to_all(fan[0], "py", 0, 0, tiled=True)] + args
    return pl.pallas_call(
        lambda *refs: collect_kernel(kept, *refs),
        out_shape=jax.ShapeDtypeStruct((32, 25, 64, 64), F32),
        grid_spec=pltpu.PrefetchScalarGridSpec(
            num_scalar_prefetch=1,
            grid=(32,),
            in_specs=[spec(VM)] * len(args),
            out_specs=pl.BlockSpec((1, 25, 64, 64), lambda n, source: (n, 0, 0, 0)),
        ),
        compiler_params=params(),
    )(source, *args)


def body(
    coupling_vals, coupling_cols, coupling_len, interp_vals, interp_cols, interp_len, owner_map
):
    size_x = lax.axis_size("px")
    size_y = lax.axis_size("py")
    mine_x = lax.axis_index("px")
    mine_y = lax.axis_index("py")
    meta = jnp.stack([mine_x, mine_y, 4 * size_y]).astype(jnp.int32)
    wide = jax.ShapeDtypeStruct((4, 64, 256), F32)
    dense, west, east, south, north, corners = pl.pallas_call(
        interp_kernel,
        out_shape=[jax.ShapeDtypeStruct((16, 64, 256), F32), wide, wide, wide, wide, wide],
        in_specs=[spec(SM)] * 3 + [spec(VM)],
        out_specs=[spec(VM)] * 6,
        scratch_shapes=[VM((16, 5, 64, 64), F32)],
        compiler_params=params(),
    )(meta, interp_cols, interp_len, interp_vals)

    def shift(value, dx, dy):
        pairs = [
            (x * size_y + y, (x + dx) * size_y + y + dy)
            for x in range(size_x)
            for y in range(size_y)
            if 0 <= x + dx < size_x and 0 <= y + dy < size_y
        ]
        return lax.ppermute(value, ("px", "py"), pairs)

    at_west = shift(east, 1, 0)
    at_east = shift(west, -1, 0)
    at_south = shift(north, 0, 1)
    at_north = shift(south, 0, -1)
    c00 = shift(corners[3], 1, 1)
    c01 = shift(corners[2], 1, -1)
    c10 = shift(corners[1], -1, 1)
    c11 = shift(corners[0], -1, -1)

    ints = lambda n: jax.ShapeDtypeStruct((n,), jnp.int32)
    deliver, extra, source, plain, ids, need = pl.pallas_call(
        lambda *refs: route_kernel(FAST_K, *refs),
        out_shape=[ints(16 * 32), ints(64), ints(32), ints(32), ints(32), ints(8)],
        in_specs=[spec(SM)] * 2,
        out_specs=[spec(SM)] * 6,
        scratch_shapes=[SM((16,), jnp.int32)],
    )(meta, owner_map.reshape(64))
    most = need
    for flip in (1, 2, 4):
        other = lax.ppermute(most, "px", [(x, x ^ flip) for x in range(size_x)])
        most = jnp.maximum(most, other)

    own, send = pl.pallas_call(
        galerkin_kernel,
        out_shape=[
            jax.ShapeDtypeStruct((6, 64, 1600), F32),
            jax.ShapeDtypeStruct((3, 64, 1280), F32),
        ],
        in_specs=[spec(SM)] * 3 + [spec(VM)] * 10,
        out_specs=[spec(VM)] * 2,
        scratch_shapes=[
            VM((16, 10, 64, 64), F32),
            VM((36, 64, 256), BF16),
            VM((36, 64, 256), BF16),
            VM((256, 1024), F32),
        ],
        compiler_params=params(),
    )(
        meta, coupling_cols, coupling_len, coupling_vals, dense,
        at_west, at_east, at_south, at_north, c00, c01, c10, c11,
    )
    got = shift(send, 1, 0)
    packed = pl.pallas_call(
        pack_kernel,
        out_shape=jax.ShapeDtypeStruct((16, 2, 8, 2176), F32),
        in_specs=[spec(VM)] * 2,
        out_specs=spec(VM),
        scratch_shapes=[VM((3, 64, 1600), F32)],
        compiler_params=params(),
    )(own, got)
    spread = lax.all_to_all(packed, "py", 0, 0, tiled=True)
    rows = lax.cond(
        most[0] <= FAST_E,
        lambda s: relay(FAST_K, FAST_E, meta, deliver, extra, source, s),
        lambda s: relay(32, 0, meta, deliver, extra, plain, s),
        spread,
    )
    return rows, ids


def solution(mesh):
    in_specs = (
        P("px", "py", None, None, None),
        P("px", "py", None),
        P("px", "py"),
        P("px", "py", None, None, None),
        P("px", "py", None),
        P("px", "py"),
        P("px", None, None, None),
    )
    out_specs = (P(("px", "py"), None, None, None), P(("px", "py")))
    return jax.shard_map(body, mesh=mesh, in_specs=in_specs, out_specs=out_specs, check_vma=False)
```

```python
import jax
import jax.numpy as jnp
from jax import lax
from jax.experimental import pallas as pl
from jax.experimental.pallas import tpu as pltpu
from jax.sharding import PartitionSpec as P

KEPT = 6
SPARES = (14, 16, 18, 22)
BUFFERS = 4
VM = pltpu.VMEM
SM = pltpu.SMEM
F32 = jnp.float32
BF16 = jnp.bfloat16
LIMIT = 60 * 1024 * 1024


def spec(space):
    return pl.BlockSpec(memory_space=space)


def params():
    return pltpu.CompilerParams(vmem_limit_bytes=LIMIT)


def split(value):
    high = value.astype(BF16)
    low = (value - high.astype(F32)).astype(BF16)
    return high, low


def dot3(left, right):
    out = jnp.dot(left[0], right[0], preferred_element_type=F32)
    out += jnp.dot(left[0], right[1], preferred_element_type=F32)
    out += jnp.dot(left[1], right[0], preferred_element_type=F32)
    return out


def interp_kernel(meta, cols, lens, vals, dense, south, north, slots):
    coarse_y = meta[2] // 2
    slots[...] = jnp.zeros_like(slots)
    for x in range(4):
        for y in range(4):
            row_x = (meta[0] * 4 + x) // 2
            row_y = (meta[1] * 4 + y) // 2
            count = lens[x, y]
            for s in range(4):
                col = cols[x, y, s]
                place = (col % coarse_y - row_y) * 2 + (col // coarse_y - row_x)
                place = jnp.where(s < count, place, 4)
                slots[x * 4 + y, place] = vals[x, y, s]
    for x in range(4):
        for y in range(4):
            j = x * 4 + y
            block = jnp.concatenate([slots[j, q] for q in range(4)], axis=1)
            dense[j] = block
            if y == 0:
                south[x] = block
            if y == 3:
                north[x] = block


NEAR = {-1: [0], 0: [0, 1], 1: [1]}
FAR = {-1: [-1], 0: [0, 1], 1: [2]}


def sheet(dx, dy):
    if dx == 0 and dy == 0:
        return slice(0, 256), slice(0, 256)
    if dy == 0:
        return (slice(0, 128) if dx < 0 else slice(128, 256)), slice(256, 384)
    if dx == 0:
        return (slice(0, 128) if dy < 0 else slice(128, 256)), slice(384, 512)
    at = ((dx > 0) * 2 + (dy > 0)) * 64
    return slice(at, at + 64), slice(512, 576)


def prepare_kernel(meta, cols, lens, vals, dense, left, turned, slots):
    fine_y = meta[2]
    slots[...] = jnp.zeros_like(slots)
    for x in range(4):
        for y in range(4):
            row_x = meta[0] * 4 + x
            row_y = meta[1] * 4 + y
            count = lens[x, y]
            for s in range(9):
                col = cols[x, y, s]
                place = (col // fine_y - row_x + 1) * 3 + (col % fine_y - row_y + 1)
                place = jnp.where(s < count, place, 9)
                slots[x * 4 + y, place] = vals[x, y, s]
    for ax in range(2):
        for ay in range(2):
            for dx in (-1, 0, 1):
                for dy in (-1, 0, 1):
                    fine_i = [(u, v) for u in NEAR[dx] for v in NEAR[dy]]
                    fine_j = [(u, v) for u in FAR[dx] for v in FAR[dy]]
                    rows, columns = sheet(dx, dy)
                    for n, (ix, iy) in enumerate(fine_i):
                        band = jnp.concatenate(
                            [
                                slots[
                                    (2 * ax + ix) * 4 + 2 * ay + iy,
                                    (u - ix + 1) * 3 + v - iy + 1,
                                ]
                                for u, v in fine_j
                            ],
                            axis=1,
                        )
                        at = slice(rows.start + n * 64, rows.start + n * 64 + 64)
                        high, low = split(band)
                        left[ax, ay, 0, at, columns] = high
                        left[ax, ay, 1, at, columns] = low
            own_p = jnp.concatenate(
                [dense[(2 * ax + u) * 4 + 2 * ay + v] for u in range(2) for v in range(2)], axis=0
            )
            high, low = split(own_p.T)
            turned[ax, ay, 0] = high
            turned[ax, ay, 1] = low


def galerkin_kernel(ax, left, turned, dense, side, at_south, at_north, *refs):
    phi, plo, wacc = refs[-3:]
    for x in range(4):
        for y in range(6):
            at_x, at_y = 2 * ax - 1 + x, y - 1
            if at_x < 0 or at_x > 3:
                block = side[y]
            elif at_y < 0:
                block = at_south[at_x]
            elif at_y > 3:
                block = at_north[at_x]
            else:
                block = dense[at_x * 4 + at_y]
            high, low = split(block)
            phi[x * 6 + y] = high
            plo[x * 6 + y] = low

    if ax == 1:
        send, part = refs[:2]
        send[...] = jnp.zeros_like(send)
        part[...] = jnp.zeros_like(part)
    else:
        part, own, out, acc = refs[:4]
        own[...] = jnp.zeros_like(own)
        acc[...] = part[...]

    for ay in range(2):
        wacc[...] = jnp.zeros_like(wacc)
        for dx in (-1, 0, 1):
            for dy in (-1, 0, 1):
                fine_i = [(u, v) for u in NEAR[dx] for v in NEAR[dy]]
                fine_j = [(u, v) for u in FAR[dx] for v in FAR[dy]]
                rows, columns = sheet(dx, dy)
                where = [(u + 1) * 6 + 2 * ay + v + 1 for u, v in fine_j]
                right = (
                    jnp.concatenate([phi[n] for n in where], axis=0),
                    jnp.concatenate([plo[n] for n in where], axis=0),
                )
                product = dot3(
                    (left[0, ay, 0, rows, columns], left[0, ay, 1, rows, columns]), right
                )
                for n, (ix, iy) in enumerate(fine_i):
                    at_row = slice((ix * 2 + iy) * 64, (ix * 2 + iy) * 64 + 64)
                    for qy in range(2):
                        at = ((dy + 1 + qy) * 4 + dx + 1) * 64
                        wacc[at_row, at : at + 128] += product[
                            n * 64 : n * 64 + 64, qy * 128 : qy * 128 + 128
                        ]
        coarse = dot3((turned[0, ay, 0], turned[0, ay, 1]), split(wacc[...]))
        for qy in range(2):
            for qx in range(2):
                rows = slice((qy * 2 + qx) * 64, (qy * 2 + qx) * 64 + 64)
                for ty in range(4):
                    piece = coarse[rows, ty * 256 : ty * 256 + 256]
                    at = ((ty + 1 - qy) * 5 + 1 - qx) * 64
                    if ax == 1 and qx == 1:
                        at = (ty + 1 - qy) * 256
                        send[ay + qy, :, at : at + 256] += piece
                    elif ax == 1:
                        part[ay + qy, :, at : at + 256] += piece
                    elif qx == 1:
                        acc[ay + qy, :, at : at + 256] += piece
                    else:
                        own[ay + qy, :, at : at + 256] += piece
    if ax == 0:
        pack_rows([acc[iy] for iy in range(3)], out, 1)


def half_tiles(piece, start, stop):
    return piece[:, start * 64 : stop * 64]


def pack_rows(row, out, ix):
    for g in range(8):
        band = [r[g * 8 : g * 8 + 8] for r in row]
        out[2 * g, ix, :, 0:768] = half_tiles(band[1], 0, 12)
        out[2 * g, ix, :, 768:1536] = half_tiles(band[2], 0, 12)
        out[2 * g, ix, :, 1536:2048] = half_tiles(band[0], 4, 12)
        out[2 * g, ix, :, 2048:2176] = jnp.zeros((8, 128), F32)
        out[2 * g + 1, ix, :, 0:768] = half_tiles(band[1], 12, 24)
        out[2 * g + 1, ix, :, 768:1536] = half_tiles(band[0], 12, 24)
        out[2 * g + 1, ix, :, 1536:1664] = jnp.concatenate(
            [half_tiles(band[1], 24, 25), half_tiles(band[0], 24, 25)], axis=1
        )
        out[2 * g + 1, ix, :, 1664:2176] = half_tiles(band[2], 12, 20)


def pack_kernel(own, got, packed, out, acc):
    for iy in range(3):
        acc[iy] = own[iy]
        for jy in range(5):
            acc[iy, :, jy * 320 : jy * 320 + 256] += got[iy, :, jy * 256 : jy * 256 + 256]
    pack_rows([acc[iy] for iy in range(3)], out, 0)


def route_kernel(meta, owners, deliver, extra, source, plain, ids, pick, count):
    peers = 16
    coarse_y = meta[2] // 2
    for e in range(peers):
        count[e] = 0
    for n in range(2 * peers):
        source[n] = -1
        plain[n] = -1
        ids[n] = -1

    def clear(n, carry):
        for m in range(8):
            deliver[n * 8 + m] = 0
        return carry

    lax.fori_loop(0, peers * 32 // 8, clear, 0)
    for n in range(64):
        extra[n] = 0

    def step(dy, spare):
        for k in range(4):
            e = owners[dy * 4 + k]
            rank = 0
            for before in range(k):
                rank += (owners[dy * 4 + before] == e).astype(jnp.int32)
            n = count[e]
            count[e] = n + 1
            deliver[e * 32 + n] = dy * 4 + k
            over = n >= KEPT
            here = jnp.where(over, KEPT + spare, n)
            extra[jnp.where(over, spare, 63)] = dy * 4 + k
            spare = jnp.where(over, spare + 1, spare)

            @pl.when(e == meta[1])
            def _():
                source[dy * 2 + rank] = here
                plain[dy * 2 + rank] = n
                ids[dy * 2 + rank] = (meta[0] * 2 + k // 2) * coarse_y + dy * 2 + k % 2

        return spare

    spare = lax.fori_loop(0, peers, step, 0)
    branch = 0
    for most in SPARES:
        branch += (spare > most).astype(jnp.int32)
    for n in range(8):
        pick[n] = branch


def put_pair(out, first, second):
    out[:, 0:768] = first[:, 0:768]
    out[:, 768:1536] = second[:, 0:768]
    out[:, 1536:1664] = jnp.concatenate([first[:, 768:832], second[:, 768:832]], axis=1)


def fan_kernel(kept, spare, meta, deliver, extra, got, *refs):
    rows = refs[-1]
    half = meta[1] % 2

    @pl.when(half == 0)
    def _():
        def step(dy, carry):
            for ix in range(2):
                rows[dy * 4 + ix * 2, :, 0:256] = jnp.zeros((8, 256), F32)
                rows[dy * 4 + ix * 2, :, 256:768] = got[dy, ix, :, 1536:2048]
                rows[dy * 4 + ix * 2 + 1, :, 0:768] = got[dy, ix, :, 0:768]

                @pl.when(dy > 0)
                def _():
                    rows[dy * 4 + ix * 2, :, 0:768] += got[dy - 1, ix, :, 768:1536]

            return carry

        lax.fori_loop(0, 16, step, 0)

    @pl.when(half == 1)
    def _():
        def step(dy, carry):
            for ix in range(2):
                last = got[dy, ix, :, 1536:1664]
                rows[dy * 4 + ix * 2 + 1, :, 0:768] = got[dy, ix, :, 0:768]
                rows[dy * 4 + ix * 2 + 1, :, 768:896] = last
                rows[dy * 4 + ix * 2, :, 0:768] = got[dy, ix, :, 768:1536]
                rows[dy * 4 + ix * 2, :, 768:832] = last[:, 64:128]

                @pl.when(dy > 0)
                def _():
                    rows[dy * 4 + ix * 2, :, 0:512] += got[dy - 1, ix, :, 1664:2176]

            return carry

        lax.fori_loop(0, 16, step, 0)

    def place(e, carry):
        for n in range(kept // 2):
            at = e * 32 + 2 * n
            put_pair(refs[0].at[e, n], rows[deliver[at]], rows[deliver[at + 1]])
        return carry

    lax.fori_loop(0, 16, place, 0)
    for n in range(spare // 2):
        put_pair(refs[1].at[n], rows[extra[2 * n]], rows[extra[2 * n + 1]])


def collect_kernel(low, high, first, source, parts, *refs):
    out, built, blank, sems = refs[-4:]

    def build(slot, at):
        pair = at // 2
        odd = at % 2
        start = pl.multiple_of(odd * 768, 128)
        for g in range(8):
            left = parts[2 * g, pair, :, pl.ds(start, 768)]
            right = parts[2 * g + 1, pair, :, pl.ds(start, 768)]
            last = parts[2 * g + 1, pair, :, 1536:1664]
            last = jnp.where(odd == 0, last[:, 0:64], last[:, 64:128])
            for n in range(25):
                if n < 12:
                    piece = left[:, n * 64 : n * 64 + 64]
                elif n < 24:
                    piece = right[:, (n - 12) * 64 : (n - 12) * 64 + 64]
                else:
                    piece = last
                built[slot, (n % 5) * 5 + n // 5, g * 8 : g * 8 + 8, :] = piece

    def wait(buffer):
        pltpu.make_async_copy(built.at[buffer], out.at[0], sems.at[buffer]).wait()

    if first:
        blank[...] = jnp.zeros_like(blank)

        def clear(slot, carry):
            @pl.when(source[slot] < 0)
            def _():
                pltpu.make_async_copy(blank, out.at[slot], sems.at[BUFFERS]).start()

            return carry

        lax.fori_loop(0, 32, clear, 0)

    def step(slot, done):
        at = source[slot]
        here = (at >= low) & (at < high)
        buffer = done % BUFFERS

        @pl.when(here & (done >= BUFFERS))
        def _():
            wait(buffer)

        @pl.when(here)
        def _():
            build(buffer, at - low)
            pltpu.make_async_copy(built.at[buffer], out.at[slot], sems.at[buffer]).start()

        return jnp.where(here, done + 1, done)

    done = lax.fori_loop(0, 32, step, 0)
    for buffer in range(BUFFERS):

        @pl.when(done > buffer)
        def _():
            wait(buffer)

    if first:

        def settle(slot, carry):
            @pl.when(source[slot] < 0)
            def _():
                pltpu.make_async_copy(blank, out.at[0], sems.at[BUFFERS]).wait()

            return carry

        lax.fori_loop(0, 32, settle, 0)


def collect(low, high, source, parts, base=None):
    args = [source, parts] + ([] if base is None else [base])
    return pl.pallas_call(
        lambda *refs: collect_kernel(low, high, base is None, *refs),
        out_shape=jax.ShapeDtypeStruct((32, 25, 64, 64), F32),
        in_specs=[spec(SM), spec(VM), spec(pl.ANY)][: len(args)],
        out_specs=spec(pl.ANY),
        scratch_shapes=[
            VM((BUFFERS, 25, 64, 64), F32),
            VM((25, 64, 64), F32),
            pltpu.SemaphoreType.DMA((BUFFERS + 1,)),
        ],
        input_output_aliases={} if base is None else {2: 0},
        compiler_params=params(),
    )(*args)


def relay(kept, spare, meta, deliver, extra, source, got):
    outs = [jax.ShapeDtypeStruct((16, kept // 2, 8, 1664), F32)]
    if spare:
        outs.append(jax.ShapeDtypeStruct((spare // 2, 8, 1664), F32))
    fan = pl.pallas_call(
        lambda *refs: fan_kernel(kept, spare, *refs),
        out_shape=outs,
        in_specs=[spec(SM)] * 3 + [spec(VM)],
        out_specs=[spec(VM)] * len(outs),
        scratch_shapes=[VM((64, 8, 896), F32)],
        compiler_params=params(),
    )(meta, deliver, extra, got)
    if spare:
        far = lax.all_gather(fan[1], "py", axis=0, tiled=False)
    near = lax.all_to_all(fan[0], "py", 0, 0, tiled=True)
    rows = collect(0, kept, source, near)
    if spare:
        rows = collect(kept, kept + spare, source, far, rows)
    return rows


def body(
    coupling_vals, coupling_cols, coupling_len, interp_vals, interp_cols, interp_len, owner_map
):
    size_x = lax.axis_size("px")
    size_y = lax.axis_size("py")
    mine_x = lax.axis_index("px")
    mine_y = lax.axis_index("py")
    meta = jnp.stack([mine_x, mine_y, 4 * size_y]).astype(jnp.int32)
    edge = jax.ShapeDtypeStruct((4, 64, 256), F32)
    dense, south, north = pl.pallas_call(
        interp_kernel,
        out_shape=[jax.ShapeDtypeStruct((16, 64, 256), F32), edge, edge],
        in_specs=[spec(SM)] * 3 + [spec(VM)],
        out_specs=[spec(VM)] * 3,
        scratch_shapes=[VM((16, 5, 64, 64), F32)],
        compiler_params=params(),
    )(meta, interp_cols, interp_len, interp_vals)

    def shift(value, axis, step):
        count = lax.axis_size(axis)
        pairs = [(i, i + step) for i in range(count) if 0 <= i + step < count]
        return lax.ppermute(value, axis, pairs)

    at_south = shift(north, "py", 1)
    at_north = shift(south, "py", -1)
    west = jnp.concatenate([at_south[:1], dense[:4], at_north[:1]], axis=0)
    east = jnp.concatenate([at_south[3:], dense[12:], at_north[3:]], axis=0)
    left, turned = pl.pallas_call(
        prepare_kernel,
        out_shape=[
            jax.ShapeDtypeStruct((2, 2, 2, 256, 640), BF16),
            jax.ShapeDtypeStruct((2, 2, 2, 256, 256), BF16),
        ],
        in_specs=[spec(SM)] * 3 + [spec(VM)] * 2,
        out_specs=[spec(VM)] * 2,
        scratch_shapes=[VM((16, 10, 64, 64), F32)],
        compiler_params=params(),
    )(meta, coupling_cols, coupling_len, coupling_vals, dense)
    west, east, left = lax.optimization_barrier((west, east, left))
    at_west = shift(east, "px", 1)
    at_east = shift(west, "px", -1)
    at_west, at_east = lax.optimization_barrier((at_west, at_east))

    ints = lambda n: jax.ShapeDtypeStruct((n,), jnp.int32)
    deliver, extra, source, plain, ids, pick = pl.pallas_call(
        route_kernel,
        out_shape=[ints(16 * 32), ints(64), ints(32), ints(32), ints(32), ints(8)],
        in_specs=[spec(SM)] * 2,
        out_specs=[spec(SM)] * 6,
        scratch_shapes=[SM((16,), jnp.int32)],
    )(meta, owner_map.reshape(64))
    branch = pick
    for flip in (1, 2, 4):
        other = lax.ppermute(branch, "px", [(x, x ^ flip) for x in range(size_x)])
        branch = jnp.maximum(branch, other)

    def galerkin(ax, side, outs, spaces, *extra_args):
        half = lambda *shape: pl.BlockSpec((1,) + shape, lambda n: (ax,) + (0,) * len(shape))
        return pl.pallas_call(
            lambda *refs: galerkin_kernel(ax, *refs),
            grid=(1,),
            out_shape=outs,
            in_specs=[half(2, 2, 256, 640), half(2, 2, 256, 256)]
            + [spec(VM)] * (4 + len(extra_args)),
            out_specs=spaces,
            scratch_shapes=([] if ax else [VM((3, 64, 1600), F32)])
            + [
                VM((24, 64, 256), BF16),
                VM((24, 64, 256), BF16),
                VM((256, 1024), F32),
            ],
            compiler_params=params(),
        )(left, turned, dense, side, at_south, at_north, *extra_args)

    row = jax.ShapeDtypeStruct((3, 64, 1600), F32)
    packed = jax.ShapeDtypeStruct((16, 2, 8, 2176), F32)
    send, part = galerkin(
        1, at_east, [jax.ShapeDtypeStruct((3, 64, 1280), F32), row], [spec(VM)] * 2
    )
    got = shift(send, "px", 1)
    own, packed1 = galerkin(0, at_west, [row, packed], [spec(VM)] * 2, part)
    packed2 = pl.pallas_call(
        pack_kernel,
        grid=(1,),
        out_shape=packed,
        in_specs=[spec(VM)] * 2 + [spec(pl.ANY)],
        out_specs=pl.BlockSpec((16, 1, 8, 2176), lambda n: (0, 0, 0, 0)),
        scratch_shapes=[VM((3, 64, 1600), F32)],
        input_output_aliases={2: 0},
        compiler_params=params(),
    )(own, got, packed1)
    spread = lax.all_to_all(packed2, "py", 0, 0, tiled=True)
    branches = [
        lambda a, most=most: relay(KEPT, most, meta, deliver, extra, source, a) for most in SPARES
    ]
    branches.append(lambda a: relay(32, 0, meta, deliver, extra, plain, a))
    rows = lax.switch(branch[0], branches, spread)
    return rows, ids


def solution(mesh):
    in_specs = (
        P("px", "py", None, None, None),
        P("px", "py", None),
        P("px", "py"),
        P("px", "py", None, None, None),
        P("px", "py", None),
        P("px", "py"),
        P("px", None, None, None),
    )
    out_specs = (P(("px", "py"), None, None, None), P(("px", "py")))
    return jax.shard_map(body, mesh=mesh, in_specs=in_specs, out_specs=out_specs, check_vma=False)
```

```python
import jax
import jax.numpy as jnp
from jax import lax
from jax.experimental import pallas as pl
from jax.experimental.pallas import tpu as pltpu
from jax.sharding import PartitionSpec as P

KEPT = 6
SPARES = (14, 16, 18, 22)
BUFFERS = 4
STARTS = (-256, 1024, 2304)
VM = pltpu.VMEM
SM = pltpu.SMEM
F32 = jnp.float32
BF16 = jnp.bfloat16
LIMIT = 60 * 1024 * 1024


def spec(space):
    return pl.BlockSpec(memory_space=space)


def params():
    return pltpu.CompilerParams(vmem_limit_bytes=LIMIT)


def split(value):
    high = value.astype(BF16)
    low = (value - high.astype(F32)).astype(BF16)
    return high, low


def dot3(left, right):
    out = jnp.dot(left[0], right[0], preferred_element_type=F32)
    out += jnp.dot(left[0], right[1], preferred_element_type=F32)
    out += jnp.dot(left[1], right[0], preferred_element_type=F32)
    return out


def interp_kernel(meta, cols, lens, vals, dense, south, north, slots):
    coarse_y = meta[2] // 2
    slots[...] = jnp.zeros_like(slots)
    for x in range(4):
        for y in range(4):
            row_x = (meta[0] * 4 + x) // 2
            row_y = (meta[1] * 4 + y) // 2
            count = lens[x, y]
            for s in range(4):
                col = cols[x, y, s]
                place = (col % coarse_y - row_y) * 2 + (col // coarse_y - row_x)
                place = jnp.where(s < count, place, 4)
                slots[x * 4 + y, place] = vals[x, y, s]
    for x in range(4):
        for y in range(4):
            j = x * 4 + y
            block = jnp.concatenate([slots[j, q] for q in range(4)], axis=1)
            dense[j] = block
            if y == 0:
                south[x] = block
            if y == 3:
                north[x] = block


NEAR = {-1: [0], 0: [0, 1], 1: [1]}
FAR = {-1: [-1], 0: [0, 1], 1: [2]}


def sheet(dx, dy):
    if dx == 0 and dy == 0:
        return slice(0, 256), slice(0, 256)
    if dy == 0:
        return (slice(0, 128) if dx < 0 else slice(128, 256)), slice(256, 384)
    if dx == 0:
        return (slice(0, 128) if dy < 0 else slice(128, 256)), slice(384, 512)
    at = ((dx > 0) * 2 + (dy > 0)) * 64
    return slice(at, at + 64), slice(512, 576)


def prepare_kernel(meta, cols, lens, vals, dense, left, turned, slots):
    fine_y = meta[2]
    slots[...] = jnp.zeros_like(slots)
    for x in range(4):
        for y in range(4):
            row_x = meta[0] * 4 + x
            row_y = meta[1] * 4 + y
            count = lens[x, y]
            for s in range(9):
                col = cols[x, y, s]
                place = (col // fine_y - row_x + 1) * 3 + (col % fine_y - row_y + 1)
                place = jnp.where(s < count, place, 9)
                slots[x * 4 + y, place] = vals[x, y, s]
    for ax in range(2):
        for ay in range(2):
            for dx in (-1, 0, 1):
                for dy in (-1, 0, 1):
                    fine_i = [(u, v) for u in NEAR[dx] for v in NEAR[dy]]
                    fine_j = [(u, v) for u in FAR[dx] for v in FAR[dy]]
                    rows, columns = sheet(dx, dy)
                    for n, (ix, iy) in enumerate(fine_i):
                        band = jnp.concatenate(
                            [
                                slots[
                                    (2 * ax + ix) * 4 + 2 * ay + iy,
                                    (u - ix + 1) * 3 + v - iy + 1,
                                ]
                                for u, v in fine_j
                            ],
                            axis=1,
                        )
                        at = slice(rows.start + n * 64, rows.start + n * 64 + 64)
                        high, low = split(band)
                        left[ax, ay, 0, at, columns] = high
                        left[ax, ay, 1, at, columns] = low
            own_p = jnp.concatenate(
                [dense[(2 * ax + u) * 4 + 2 * ay + v] for u in range(2) for v in range(2)], axis=0
            )
            high, low = split(own_p.T)
            turned[ax, ay, 0] = high
            turned[ax, ay, 1] = low


def galerkin_kernel(ax, left, turned, dense, side, at_south, at_north, *refs):
    phi, plo, wacc = refs[-3:]
    for x in range(4):
        for y in range(6):
            at_x, at_y = 2 * ax - 1 + x, y - 1
            if at_x < 0 or at_x > 3:
                block = side[y]
            elif at_y < 0:
                block = at_south[at_x]
            elif at_y > 3:
                block = at_north[at_x]
            else:
                block = dense[at_x * 4 + at_y]
            high, low = split(block)
            phi[x * 6 + y] = high
            plo[x * 6 + y] = low

    if ax == 1:
        send, part = refs[:2]
        send[...] = jnp.zeros_like(send)
        part[...] = jnp.zeros_like(part)
    else:
        part, own, out, acc = refs[:4]
        own[...] = jnp.zeros_like(own)
        acc[...] = part[...]

    for ay in range(2):
        wacc[...] = jnp.zeros_like(wacc)
        for dx in (-1, 0, 1):
            for dy in (-1, 0, 1):
                fine_i = [(u, v) for u in NEAR[dx] for v in NEAR[dy]]
                fine_j = [(u, v) for u in FAR[dx] for v in FAR[dy]]
                rows, columns = sheet(dx, dy)
                where = [(u + 1) * 6 + 2 * ay + v + 1 for u, v in fine_j]
                right = (
                    jnp.concatenate([phi[n] for n in where], axis=0),
                    jnp.concatenate([plo[n] for n in where], axis=0),
                )
                product = dot3(
                    (left[0, ay, 0, rows, columns], left[0, ay, 1, rows, columns]), right
                )
                for n, (ix, iy) in enumerate(fine_i):
                    at_row = slice((ix * 2 + iy) * 64, (ix * 2 + iy) * 64 + 64)
                    for qy in range(2):
                        at = ((dy + 1 + qy) * 4 + dx + 1) * 64
                        wacc[at_row, at : at + 128] += product[
                            n * 64 : n * 64 + 64, qy * 128 : qy * 128 + 128
                        ]
        coarse = dot3((turned[0, ay, 0], turned[0, ay, 1]), split(wacc[...]))
        for qy in range(2):
            for qx in range(2):
                rows = slice((qy * 2 + qx) * 64, (qy * 2 + qx) * 64 + 64)
                for ty in range(4):
                    piece = coarse[rows, ty * 256 : ty * 256 + 256]
                    at = ((ty + 1 - qy) * 5 + 1 - qx) * 64
                    if ax == 1 and qx == 1:
                        at = STARTS[ay + qy] + (ty + 1 - qy) * 256
                        send[:, at : at + 256] += piece
                    elif ax == 1:
                        part[ay + qy, :, at : at + 256] += piece
                    elif qx == 1:
                        acc[ay + qy, :, at : at + 256] += piece
                    else:
                        own[ay + qy, :, at : at + 256] += piece
    if ax == 0:
        pack_rows([acc[iy] for iy in range(3)], out, 1)


def half_tiles(piece, start, stop):
    return piece[:, start * 64 : stop * 64]


def pack_rows(row, out, ix):
    for g in range(8):
        band = [r[g * 8 : g * 8 + 8] for r in row]
        out[2 * g, ix, :, 0:768] = half_tiles(band[1], 0, 12)
        out[2 * g, ix, :, 768:1536] = half_tiles(band[2], 0, 12)
        out[2 * g, ix, :, 1536:2048] = half_tiles(band[0], 4, 12)
        out[2 * g, ix, :, 2048:2176] = jnp.zeros((8, 128), F32)
        out[2 * g + 1, ix, :, 0:768] = half_tiles(band[1], 12, 24)
        out[2 * g + 1, ix, :, 768:1536] = half_tiles(band[0], 12, 24)
        out[2 * g + 1, ix, :, 1536:1664] = jnp.concatenate(
            [half_tiles(band[1], 24, 25), half_tiles(band[0], 24, 25)], axis=1
        )
        out[2 * g + 1, ix, :, 1664:2176] = half_tiles(band[2], 12, 20)


def pack_kernel(own, got, packed, out, acc):
    for iy in range(3):
        acc[iy] = own[iy]
        for jy in range(iy == 0, 5 - (iy == 2)):
            at = STARTS[iy] + jy * 256
            acc[iy, :, jy * 320 : jy * 320 + 256] += got[:, at : at + 256]
    pack_rows([acc[iy] for iy in range(3)], out, 0)


def route_kernel(meta, owners, deliver, extra, source, plain, ids, pick, count):
    peers = 16
    coarse_y = meta[2] // 2
    for e in range(peers):
        count[e] = 0
    for n in range(2 * peers):
        source[n] = -1
        plain[n] = -1
        ids[n] = -1

    def clear(n, carry):
        for m in range(8):
            deliver[n * 8 + m] = 0
        return carry

    lax.fori_loop(0, peers * 32 // 8, clear, 0)
    for n in range(64):
        extra[n] = 0

    def step(dy, spare):
        for k in range(4):
            e = owners[dy * 4 + k]
            rank = 0
            for before in range(k):
                rank += (owners[dy * 4 + before] == e).astype(jnp.int32)
            n = count[e]
            count[e] = n + 1
            deliver[e * 32 + n] = dy * 4 + k
            over = n >= KEPT
            here = jnp.where(over, KEPT + spare, n)
            extra[jnp.where(over, spare, 63)] = dy * 4 + k
            spare = jnp.where(over, spare + 1, spare)

            @pl.when(e == meta[1])
            def _():
                source[dy * 2 + rank] = here
                plain[dy * 2 + rank] = n
                ids[dy * 2 + rank] = (meta[0] * 2 + k // 2) * coarse_y + dy * 2 + k % 2

        return spare

    spare = lax.fori_loop(0, peers, step, 0)
    branch = 0
    for most in SPARES:
        branch += (spare > most).astype(jnp.int32)
    for n in range(8):
        pick[n] = branch


def put_pair(out, first, second):
    out[:, 0:768] = first[:, 0:768]
    out[:, 768:1536] = second[:, 0:768]
    out[:, 1536:1664] = jnp.concatenate([first[:, 768:832], second[:, 768:832]], axis=1)


def fan_kernel(kept, spare, meta, deliver, extra, got, *refs):
    rows = refs[-1]
    half = meta[1] % 2

    @pl.when(half == 0)
    def _():
        def step(dy, carry):
            for ix in range(2):
                rows[dy * 4 + ix * 2, :, 0:256] = jnp.zeros((8, 256), F32)
                rows[dy * 4 + ix * 2, :, 256:768] = got[dy, ix, :, 1536:2048]
                rows[dy * 4 + ix * 2 + 1, :, 0:768] = got[dy, ix, :, 0:768]

                @pl.when(dy > 0)
                def _():
                    rows[dy * 4 + ix * 2, :, 0:768] += got[dy - 1, ix, :, 768:1536]

            return carry

        lax.fori_loop(0, 16, step, 0)

    @pl.when(half == 1)
    def _():
        def step(dy, carry):
            for ix in range(2):
                last = got[dy, ix, :, 1536:1664]
                rows[dy * 4 + ix * 2 + 1, :, 0:768] = got[dy, ix, :, 0:768]
                rows[dy * 4 + ix * 2 + 1, :, 768:896] = last
                rows[dy * 4 + ix * 2, :, 0:768] = got[dy, ix, :, 768:1536]
                rows[dy * 4 + ix * 2, :, 768:832] = last[:, 64:128]

                @pl.when(dy > 0)
                def _():
                    rows[dy * 4 + ix * 2, :, 0:512] += got[dy - 1, ix, :, 1664:2176]

            return carry

        lax.fori_loop(0, 16, step, 0)

    def place(e, carry):
        for n in range(kept // 2):
            at = e * 32 + 2 * n
            put_pair(refs[0].at[e, n], rows[deliver[at]], rows[deliver[at + 1]])
        return carry

    lax.fori_loop(0, 16, place, 0)
    for n in range(spare // 2):
        put_pair(refs[1].at[n], rows[extra[2 * n]], rows[extra[2 * n + 1]])


def collect_kernel(low, high, first, source, parts, *refs):
    out, built, blank, sems = refs[-4:]

    def build(slot, at):
        pair = at // 2
        odd = at % 2
        start = pl.multiple_of(odd * 768, 128)
        for g in range(8):
            left = parts[2 * g, pair, :, pl.ds(start, 768)]
            right = parts[2 * g + 1, pair, :, pl.ds(start, 768)]
            last = parts[2 * g + 1, pair, :, 1536:1664]
            last = jnp.where(odd == 0, last[:, 0:64], last[:, 64:128])
            for n in range(25):
                if n < 12:
                    piece = left[:, n * 64 : n * 64 + 64]
                elif n < 24:
                    piece = right[:, (n - 12) * 64 : (n - 12) * 64 + 64]
                else:
                    piece = last
                built[slot, (n % 5) * 5 + n // 5, g * 8 : g * 8 + 8, :] = piece

    def wait(buffer):
        pltpu.make_async_copy(built.at[buffer], out.at[0], sems.at[buffer]).wait()

    if first:
        blank[...] = jnp.zeros_like(blank)

        def clear(slot, carry):
            @pl.when(source[slot] < 0)
            def _():
                pltpu.make_async_copy(blank, out.at[slot], sems.at[BUFFERS]).start()

            return carry

        lax.fori_loop(0, 32, clear, 0)

    def step(slot, done):
        at = source[slot]
        here = (at >= low) & (at < high)
        buffer = done % BUFFERS

        @pl.when(here & (done >= BUFFERS))
        def _():
            wait(buffer)

        @pl.when(here)
        def _():
            build(buffer, at - low)
            pltpu.make_async_copy(built.at[buffer], out.at[slot], sems.at[buffer]).start()

        return jnp.where(here, done + 1, done)

    done = lax.fori_loop(0, 32, step, 0)
    for buffer in range(BUFFERS):

        @pl.when(done > buffer)
        def _():
            wait(buffer)

    if first:

        def settle(slot, carry):
            @pl.when(source[slot] < 0)
            def _():
                pltpu.make_async_copy(blank, out.at[0], sems.at[BUFFERS]).wait()

            return carry

        lax.fori_loop(0, 32, settle, 0)


def collect(low, high, source, parts, base=None):
    args = [source, parts] + ([] if base is None else [base])
    return pl.pallas_call(
        lambda *refs: collect_kernel(low, high, base is None, *refs),
        out_shape=jax.ShapeDtypeStruct((32, 25, 64, 64), F32),
        in_specs=[spec(SM), spec(VM), spec(pl.ANY)][: len(args)],
        out_specs=spec(pl.ANY),
        scratch_shapes=[
            VM((BUFFERS, 25, 64, 64), F32),
            VM((25, 64, 64), F32),
            pltpu.SemaphoreType.DMA((BUFFERS + 1,)),
        ],
        input_output_aliases={} if base is None else {2: 0},
        compiler_params=params(),
    )(*args)


def relay(kept, spare, meta, deliver, extra, source, got):
    outs = [jax.ShapeDtypeStruct((16, kept // 2, 8, 1664), F32)]
    if spare:
        outs.append(jax.ShapeDtypeStruct((spare // 2, 8, 1664), F32))
    fan = pl.pallas_call(
        lambda *refs: fan_kernel(kept, spare, *refs),
        out_shape=outs,
        in_specs=[spec(SM)] * 3 + [spec(VM)],
        out_specs=[spec(VM)] * len(outs),
        scratch_shapes=[VM((64, 8, 896), F32)],
        compiler_params=params(),
    )(meta, deliver, extra, got)
    if spare:
        far = lax.all_gather(fan[1], "py", axis=0, tiled=False)
    near = lax.all_to_all(fan[0], "py", 0, 0, tiled=True)
    rows = collect(0, kept, source, near)
    if spare:
        rows = collect(kept, kept + spare, source, far, rows)
    return rows


def body(
    coupling_vals, coupling_cols, coupling_len, interp_vals, interp_cols, interp_len, owner_map
):
    size_x = lax.axis_size("px")
    size_y = lax.axis_size("py")
    mine_x = lax.axis_index("px")
    mine_y = lax.axis_index("py")
    meta = jnp.stack([mine_x, mine_y, 4 * size_y]).astype(jnp.int32)
    edge = jax.ShapeDtypeStruct((4, 64, 256), F32)
    dense, south, north = pl.pallas_call(
        interp_kernel,
        out_shape=[jax.ShapeDtypeStruct((16, 64, 256), F32), edge, edge],
        in_specs=[spec(SM)] * 3 + [spec(VM)],
        out_specs=[spec(VM)] * 3,
        scratch_shapes=[VM((16, 5, 64, 64), F32)],
        compiler_params=params(),
    )(meta, interp_cols, interp_len, interp_vals)

    def shift(value, axis, step):
        count = lax.axis_size(axis)
        pairs = [(i, i + step) for i in range(count) if 0 <= i + step < count]
        return lax.ppermute(value, axis, pairs)

    at_south = shift(north, "py", 1)
    at_north = shift(south, "py", -1)
    west = jnp.concatenate([at_south[:1], dense[:4], at_north[:1]], axis=0)
    east = jnp.concatenate([at_south[3:], dense[12:], at_north[3:]], axis=0)
    left, turned = pl.pallas_call(
        prepare_kernel,
        out_shape=[
            jax.ShapeDtypeStruct((2, 2, 2, 256, 640), BF16),
            jax.ShapeDtypeStruct((2, 2, 2, 256, 256), BF16),
        ],
        in_specs=[spec(SM)] * 3 + [spec(VM)] * 2,
        out_specs=[spec(VM)] * 2,
        scratch_shapes=[VM((16, 10, 64, 64), F32)],
        compiler_params=params(),
    )(meta, coupling_cols, coupling_len, coupling_vals, dense)
    west, east, left = lax.optimization_barrier((west, east, left))
    at_west = shift(east, "px", 1)
    at_east = shift(west, "px", -1)
    at_west, at_east = lax.optimization_barrier((at_west, at_east))

    ints = lambda n: jax.ShapeDtypeStruct((n,), jnp.int32)
    deliver, extra, source, plain, ids, pick = pl.pallas_call(
        route_kernel,
        out_shape=[ints(16 * 32), ints(64), ints(32), ints(32), ints(32), ints(8)],
        in_specs=[spec(SM)] * 2,
        out_specs=[spec(SM)] * 6,
        scratch_shapes=[SM((16,), jnp.int32)],
    )(meta, owner_map.reshape(64))
    branch = pick
    for flip in (1, 2, 4):
        other = lax.ppermute(branch, "px", [(x, x ^ flip) for x in range(size_x)])
        branch = jnp.maximum(branch, other)

    def galerkin(ax, side, outs, spaces, *extra_args):
        half = lambda *shape: pl.BlockSpec((1,) + shape, lambda n: (ax,) + (0,) * len(shape))
        return pl.pallas_call(
            lambda *refs: galerkin_kernel(ax, *refs),
            grid=(1,),
            out_shape=outs,
            in_specs=[half(2, 2, 256, 640), half(2, 2, 256, 256)]
            + [spec(VM)] * (4 + len(extra_args)),
            out_specs=spaces,
            scratch_shapes=([] if ax else [VM((3, 64, 1600), F32)])
            + [
                VM((24, 64, 256), BF16),
                VM((24, 64, 256), BF16),
                VM((256, 1024), F32),
            ],
            compiler_params=params(),
        )(left, turned, dense, side, at_south, at_north, *extra_args)

    row = jax.ShapeDtypeStruct((3, 64, 1600), F32)
    packed = jax.ShapeDtypeStruct((16, 2, 8, 2176), F32)
    send, part = galerkin(
        1, at_east, [jax.ShapeDtypeStruct((64, 3328), F32), row], [spec(VM)] * 2
    )
    got = shift(send, "px", 1)
    own, packed1 = galerkin(0, at_west, [row, packed], [spec(VM)] * 2, part)
    packed2 = pl.pallas_call(
        pack_kernel,
        grid=(1,),
        out_shape=packed,
        in_specs=[spec(VM)] * 2 + [spec(pl.ANY)],
        out_specs=pl.BlockSpec((16, 1, 8, 2176), lambda n: (0, 0, 0, 0)),
        scratch_shapes=[VM((3, 64, 1600), F32)],
        input_output_aliases={2: 0},
        compiler_params=params(),
    )(own, got, packed1)
    spread = lax.all_to_all(packed2, "py", 0, 0, tiled=True)
    branches = [
        lambda a, most=most: relay(KEPT, most, meta, deliver, extra, source, a) for most in SPARES
    ]
    branches.append(lambda a: relay(32, 0, meta, deliver, extra, plain, a))
    rows = lax.switch(branch[0], branches, spread)
    return rows, ids


def solution(mesh):
    in_specs = (
        P("px", "py", None, None, None),
        P("px", "py", None),
        P("px", "py"),
        P("px", "py", None, None, None),
        P("px", "py", None),
        P("px", "py"),
        P("px", None, None, None),
    )
    out_specs = (P(("px", "py"), None, None, None), P(("px", "py")))
    return jax.shard_map(body, mesh=mesh, in_specs=in_specs, out_specs=out_specs, check_vma=False)
```
